32 devices in a mesh: wide: 8 (over z, y), narrow: 4 (over x, core).
Axes of the slice: x: 2, y: 2, z: 4, core: 2. Of those that a mesh axis runs over, the one named last changes fastest.
Arguments:
- matrix_panel: float32 [8, 4194304], P(None, ('wide', 'narrow')), may hold values from -6 to 6
- sign_bits: int32 [4194304], P(('wide', 'narrow')), may hold values from 0 to 1
Outputs:
- mixed_panel: float32 [8, 4194304], P(None, ('wide', 'narrow'))
The draws below stay inside these ranges and needn't reach their ends.
All inputs are finite; a program needn't handle non-finite values.
Results may differ from the reference program's by a relative error of at most 0.000086.
Values sent between devices are 32-bit elements; how exact they have to be, the bound alone decides.
A program may use at most 64 MiB of HBM per device.

```python
import math
import jax
import jax.numpy as jnp

COLS = 8
LENGTH = 4194304


def set_ends(entries, key, least, largest):
    shape = entries.shape
    spot = [jax.random.randint(jax.random.fold_in(key, axis), (), 0, shape[axis]) for axis in range(len(shape))]
    entries = entries.at[tuple(spot)].set(least)
    longest = shape.index(max(shape))
    spot[longest] = (spot[longest] + 1) % shape[longest]
    return entries.at[tuple(spot)].set(largest)


def level_of(stream_key, shape, pieces, smallest, largest):
    def one(position, parts):
        steps = jax.random.uniform(jax.random.fold_in(jax.random.fold_in(stream_key, 6), position), (parts,), jnp.float32, smallest / len(pieces), largest / len(pieces))
        return jnp.repeat(jnp.exp(steps), shape[position] // parts).reshape((-1,) + (1,) * (len(shape) - position - 1))

    gain = one(*pieces[0])
    for cut in pieces[1:]:
        gain = gain * one(*cut)
    return gain


def scatter_about(key, shape, deviation, limit, split=(), kind=jnp.bfloat16):
    loudness = level_of(key, shape, split, -0.22, 0.18) if split else 1.0
    drawn = jax.random.normal(key, shape, jnp.float32) * deviation * loudness
    return jnp.minimum(jnp.maximum(drawn, -limit), limit).astype(kind)


def setup_inputs(seed: int = 0) -> dict:
    key_list = jax.random.split(jax.random.key(seed), 3)
    matrix_panel = scatter_about(key_list[0], (COLS, LENGTH), 1.0, 6.0, ((1, 32),), jnp.float32)
    sign_bits = set_ends(jax.random.randint(key_list[1], (LENGTH,), 0, 2), jax.random.fold_in(key_list[1], 1), 0, 1).astype(jnp.int32)
    return dict(matrix_panel=matrix_panel, sign_bits=sign_bits)


def reference(matrix_panel, sign_bits):
    signed = matrix_panel * (2 * sign_bits - 1).astype(jnp.float32)[None, :]
    columns, length = signed.shape
    levels = int(length).bit_length() - 1
    current = signed
    half = 1
    for level in range(levels):
        shaped = current.reshape(columns, length // (2 * half), 2, half)
        first = shaped[:, :, 0, :]
        second = shaped[:, :, 1, :]
        current = jnp.stack([first + second, first - second], axis=2).reshape(columns, length)
        half = half * 2
    return current * jnp.float32(1.0 / math.sqrt(length))
```

```python
import functools
import math

import jax
import jax.numpy as jnp
from jax import lax
from jax.experimental import pallas as pl
from jax.experimental.pallas import tpu as pltpu
from jax.sharding import PartitionSpec as P

LANES = 128
CHUNKS = 2
RADIX = 32
MESH = pl.DeviceIdType.MESH


def xor(first, second, count):
    total = 0
    for level in range(count.bit_length() - 1):
        one = lax.rem(lax.div(first, 1 << level), 2)
        two = lax.rem(lax.div(second, 1 << level), 2)
        total = total + (one + two - 2 * one * two) * (1 << level)
    return total


def butterflies(values):
    values = list(values)
    half = 1
    while half < len(values):
        for low in range(len(values)):
            if not low & half:
                a, b = values[low], values[low | half]
                values[low], values[low | half] = a + b, a - b
        half *= 2
    return values


def lane_table():
    rows = lax.broadcasted_iota(jnp.int32, (LANES, LANES), 0)
    cols = lax.broadcasted_iota(jnp.int32, (LANES, LANES), 1)
    parity = rows & cols
    for shift in (4, 2, 1):
        parity = parity ^ (parity >> shift)
    return (1 - 2 * (parity & 1)).astype(jnp.float32).astype(jnp.bfloat16)


def mix_slots(load, store, count, scale=None):
    if count <= RADIX:
        values = butterflies([load(i) for i in range(count)])
        for i, value in enumerate(values):
            store(i, value if scale is None else value * scale)
        return
    high = count // RADIX
    held = []
    for group in range(high):
        held.append(butterflies([load(group * RADIX + i) for i in range(RADIX)]))
    for i in range(RADIX):
        values = butterflies([held[group][i] for group in range(high)])
        for group, value in enumerate(values):
            store(group * RADIX + i, value if scale is None else value * scale)


def kernel(wide, narrow, chunks, scale, x_ref, s_ref, o_ref,
           ahead, landed, mixed, back, table,
           ahead_sem, landed_sem, mixed_sem, back_sem):
    count = wide * narrow
    block = x_ref.shape[1] // count
    part = block // chunks
    tiles = part // LANES
    me = lax.axis_index("wide") * narrow + lax.axis_index("narrow")

    def device(index):
        return (lax.div(index, narrow), lax.rem(index, narrow))

    def peer(step):
        half = count // 2
        flip = lax.div(step, 2)
        even = 1 - lax.rem(step, 2)
        return xor(me, flip + even * half + (1 - even), count)

    barrier = pltpu.get_barrier_semaphore()

    def greet(step, carry):
        pl.semaphore_signal(barrier, inc=1, device_id=device(peer(step)), device_id_type=MESH)
        return carry

    lax.fori_loop(0, count - 1, greet, 0)

    table[...] = lane_table()

    def low_bits(index):
        first = pl.multiple_of(index * block, block)
        first_tile = index * (block // LANES)
        values = []
        for t in range(block // LANES):
            sign = (2 * s_ref[pl.ds(first_tile + t, 1), :] - 1).astype(jnp.float32)
            values.append(x_ref[:, pl.ds(pl.multiple_of(first + t * LANES, LANES), LANES)] * sign)
        flat = jnp.concatenate(butterflies(values), axis=0)
        upper = flat.astype(jnp.bfloat16)
        lower = (flat - upper.astype(jnp.float32)).astype(jnp.bfloat16)
        out = jnp.dot(upper, table[...], preferred_element_type=jnp.float32)
        return out + jnp.dot(lower, table[...], preferred_element_type=jnp.float32)

    def keep(ref, index, value):
        for t in range(block // LANES):
            lane = (t % tiles) * LANES
            ref[t // tiles, index, :, lane:lane + LANES] = value[t * 8:(t + 1) * 8, :]

    keep(landed, me, low_bits(me))
    pl.semaphore_wait(barrier, count - 1)

    for chunk in range(chunks):
        def send_ahead(step, carry, chunk=chunk):
            to = peer(step)
            if chunk == 0:
                keep(ahead, to, low_bits(to))
            pltpu.make_async_remote_copy(
                src_ref=ahead.at[chunk, to],
                dst_ref=landed.at[chunk, me],
                send_sem=ahead_sem.at[chunk],
                recv_sem=landed_sem.at[chunk],
                device_id=device(to),
                device_id_type=MESH,
            ).start()
            return carry

        lax.fori_loop(0, count - 1, send_ahead, 0)

    def wait_bytes(ref, chunk, sem):
        spot = ref.at[chunk, pl.ds(0, count - 1)]
        pltpu.make_async_copy(spot, spot, sem.at[chunk]).wait()

    for chunk in range(chunks):
        wait_bytes(landed, chunk, landed_sem)

        def mix(t, carry, chunk=chunk):
            lanes = pl.ds(pl.multiple_of(t * LANES, LANES), LANES)

            def store(i, value):
                mixed[chunk, i, :, lanes] = value

            mix_slots(lambda i: landed[chunk, i, :, lanes], store, count)
            return carry

        lax.fori_loop(0, tiles, mix, 0)

        def send_back(step, carry, chunk=chunk):
            to = peer(step)
            pltpu.make_async_remote_copy(
                src_ref=mixed.at[chunk, to],
                dst_ref=back.at[chunk, me],
                send_sem=mixed_sem.at[chunk],
                recv_sem=back_sem.at[chunk],
                device_id=device(to),
                device_id_type=MESH,
            ).start()
            return carry

        lax.fori_loop(0, count - 1, send_back, 0)
        back[chunk, me] = mixed[chunk, me]

    for chunk in range(chunks):
        wait_bytes(back, chunk, back_sem)

        def finish(t, carry, chunk=chunk):
            lanes = pl.ds(pl.multiple_of(t * LANES, LANES), LANES)

            def store(i, value):
                start = pl.multiple_of(i * block + chunk * part + t * LANES, LANES)
                o_ref[:, pl.ds(start, LANES)] = value

            mix_slots(lambda i: back[chunk, i, :, lanes], store, count, scale)
            return carry

        lax.fori_loop(0, tiles, finish, 0)

    for chunk in range(chunks):
        wait_bytes(ahead, chunk, ahead_sem)
        wait_bytes(mixed, chunk, mixed_sem)


def body(wide, narrow, matrix_panel, sign_bits):
    columns, length = matrix_panel.shape
    count = wide * narrow
    part = length // (count * CHUNKS)
    scale = 1.0 / math.sqrt(length * count)
    slots = pltpu.VMEM((CHUNKS, count, columns, part), jnp.float32)
    return pl.pallas_call(
        functools.partial(kernel, wide, narrow, CHUNKS, scale),
        out_shape=jax.ShapeDtypeStruct((columns, length), jnp.float32),
        in_specs=[pl.BlockSpec(memory_space=pltpu.VMEM)] * 2,
        out_specs=pl.BlockSpec(memory_space=pltpu.VMEM),
        scratch_shapes=[slots] * 4
        + [pltpu.VMEM((LANES, LANES), jnp.bfloat16)]
        + [pltpu.SemaphoreType.DMA((CHUNKS,))] * 4,
        compiler_params=pltpu.CompilerParams(
            collective_id=0, has_side_effects=True, vmem_limit_bytes=48 * 1024 * 1024
        ),
        cost_estimate=pl.CostEstimate(
            flops=4 * columns * length * LANES,
            bytes_accessed=8 * columns * length,
            transcendentals=0,
        ),
    )(matrix_panel, sign_bits.reshape(length // LANES, LANES))


def solution(mesh):
    in_specs = (P(None, ("wide", "narrow")), P(("wide", "narrow")))
    out_specs = P(None, ("wide", "narrow"))
    shape = dict(mesh.shape)
    return jax.shard_map(
        functools.partial(body, shape["wide"], shape["narrow"]),
        mesh=mesh, in_specs=in_specs, out_specs=out_specs, check_vma=False,
    )
```

```python
import functools
import math

import jax
import jax.numpy as jnp
from jax import lax
from jax.experimental import pallas as pl
from jax.experimental.pallas import tpu as pltpu
from jax.sharding import PartitionSpec as P

LANES = 128
CHUNKS = 4
RADIX = 32
MESH = pl.DeviceIdType.MESH


def xor(first, second, count):
    total = 0
    for level in range(count.bit_length() - 1):
        one = lax.rem(lax.div(first, 1 << level), 2)
        two = lax.rem(lax.div(second, 1 << level), 2)
        total = total + (one + two - 2 * one * two) * (1 << level)
    return total


def butterflies(values):
    values = list(values)
    half = 1
    while half < len(values):
        for low in range(len(values)):
            if not low & half:
                a, b = values[low], values[low | half]
                values[low], values[low | half] = a + b, a - b
        half *= 2
    return values


def lane_table():
    rows = lax.broadcasted_iota(jnp.int32, (LANES, LANES), 0)
    cols = lax.broadcasted_iota(jnp.int32, (LANES, LANES), 1)
    parity = rows & cols
    for shift in (4, 2, 1):
        parity = parity ^ (parity >> shift)
    return (1 - 2 * (parity & 1)).astype(jnp.float32).astype(jnp.bfloat16)


def mix_slots(load, store, count, scale=None):
    if count <= RADIX:
        values = butterflies([load(i) for i in range(count)])
        for i, value in enumerate(values):
            store(i, value if scale is None else value * scale)
        return
    high = count // RADIX
    held = []
    for group in range(high):
        held.append(butterflies([load(group * RADIX + i) for i in range(RADIX)]))
    for i in range(RADIX):
        values = butterflies([held[group][i] for group in range(high)])
        for group, value in enumerate(values):
            store(group * RADIX + i, value if scale is None else value * scale)


def kernel(wide, narrow, chunks, scale, x_hbm, s_hbm, o_ref,
           x_ref, s_ref, ahead, landed, mixed, back, table,
           x_sem, s_sem, ahead_sem, landed_sem, mixed_sem, back_sem):
    count = wide * narrow
    block = x_ref.shape[1] // count
    part = block // chunks
    tiles = part // LANES
    me = lax.axis_index("wide") * narrow + lax.axis_index("narrow")

    def device(index):
        return (lax.div(index, narrow), lax.rem(index, narrow))

    def peer(step):
        half = count // 2
        flip = lax.div(step, 2)
        even = 1 - lax.rem(step, 2)
        return xor(me, flip + even * half + (1 - even), count)

    def fetch(index):
        spot = (slice(None), pl.ds(pl.multiple_of(index * block, block), block))
        return pltpu.make_async_copy(x_hbm.at[spot], x_ref.at[spot], x_sem.at[index])

    signs = pltpu.make_async_copy(s_hbm, s_ref, s_sem)
    signs.start()

    def fetch_peer(step, carry):
        fetch(peer(step)).start()
        return carry

    lax.fori_loop(0, count - 1, fetch_peer, 0)
    fetch(me).start()

    barrier = pltpu.get_barrier_semaphore()

    def greet(step, carry):
        pl.semaphore_signal(barrier, inc=1, device_id=device(peer(step)), device_id_type=MESH)
        return carry

    lax.fori_loop(0, count - 1, greet, 0)

    table[...] = lane_table()

    def low_bits(index):
        fetch(index).wait()
        first = pl.multiple_of(index * block, block)
        first_tile = index * (block // LANES)
        values = []
        for t in range(block // LANES):
            sign = (2 * s_ref[pl.ds(first_tile + t, 1), :] - 1).astype(jnp.float32)
            values.append(x_ref[:, pl.ds(pl.multiple_of(first + t * LANES, LANES), LANES)] * sign)
        flat = jnp.concatenate(butterflies(values), axis=0)
        upper = flat.astype(jnp.bfloat16)
        lower = (flat - upper.astype(jnp.float32)).astype(jnp.bfloat16)
        out = jnp.dot(upper, table[...], preferred_element_type=jnp.float32)
        return out + jnp.dot(lower, table[...], preferred_element_type=jnp.float32)

    def keep(ref, index, value):
        for t in range(block // LANES):
            lane = (t % tiles) * LANES
            ref[t // tiles, index, :, lane:lane + LANES] = value[t * 8:(t + 1) * 8, :]

    signs.wait()
    keep(ahead, peer(0), low_bits(peer(0)))
    pl.semaphore_wait(barrier, count - 1)

    def send_ahead(chunk, step):
        to = peer(step)
        pltpu.make_async_remote_copy(
            src_ref=ahead.at[chunk, to],
            dst_ref=landed.at[chunk, me],
            send_sem=ahead_sem.at[chunk],
            recv_sem=landed_sem.at[chunk],
            device_id=device(to),
            device_id_type=MESH,
        ).start()

    def send_then_work(step, carry):
        send_ahead(0, step)
        later = peer(step + 1)
        keep(ahead, later, low_bits(later))
        return carry

    lax.fori_loop(0, count - 2, send_then_work, 0)
    send_ahead(0, count - 2)

    for chunk in range(1, chunks):
        def send(step, carry, chunk=chunk):
            send_ahead(chunk, step)
            return carry

        lax.fori_loop(0, count - 1, send, 0)

    keep(landed, me, low_bits(me))

    def wait_bytes(ref, chunk, sem):
        spot = ref.at[chunk, pl.ds(0, count - 1)]
        pltpu.make_async_copy(spot, spot, sem.at[chunk]).wait()

    for chunk in range(chunks):
        wait_bytes(landed, chunk, landed_sem)

        def mix(t, carry, chunk=chunk):
            lanes = pl.ds(pl.multiple_of(t * LANES, LANES), LANES)

            def store(i, value):
                mixed[chunk, i, :, lanes] = value

            mix_slots(lambda i: landed[chunk, i, :, lanes], store, count)
            return carry

        lax.fori_loop(0, tiles, mix, 0)

        def send_back(step, carry, chunk=chunk):
            to = peer(step)
            pltpu.make_async_remote_copy(
                src_ref=mixed.at[chunk, to],
                dst_ref=back.at[chunk, me],
                send_sem=mixed_sem.at[chunk],
                recv_sem=back_sem.at[chunk],
                device_id=device(to),
                device_id_type=MESH,
            ).start()
            return carry

        lax.fori_loop(0, count - 1, send_back, 0)
        back[chunk, me] = mixed[chunk, me]

    for chunk in range(chunks):
        wait_bytes(back, chunk, back_sem)

        def finish(t, carry, chunk=chunk):
            lanes = pl.ds(pl.multiple_of(t * LANES, LANES), LANES)

            def store(i, value):
                start = pl.multiple_of(i * block + chunk * part + t * LANES, LANES)
                o_ref[:, pl.ds(start, LANES)] = value

            mix_slots(lambda i: back[chunk, i, :, lanes], store, count, scale)
            return carry

        lax.fori_loop(0, tiles, finish, 0)

    for chunk in range(chunks):
        wait_bytes(ahead, chunk, ahead_sem)
        wait_bytes(mixed, chunk, mixed_sem)


def body(wide, narrow, matrix_panel, sign_bits):
    columns, length = matrix_panel.shape
    count = wide * narrow
    part = length // (count * CHUNKS)
    scale = 1.0 / math.sqrt(length * count)
    slots = pltpu.VMEM((CHUNKS, count, columns, part), jnp.float32)
    return pl.pallas_call(
        functools.partial(kernel, wide, narrow, CHUNKS, scale),
        out_shape=jax.ShapeDtypeStruct((columns, length), jnp.float32),
        in_specs=[pl.BlockSpec(memory_space=pltpu.HBM)] * 2,
        out_specs=pl.BlockSpec(memory_space=pltpu.VMEM),
        scratch_shapes=[
            pltpu.VMEM((columns, length), jnp.float32),
            pltpu.VMEM((length // LANES, LANES), jnp.int32),
        ]
        + [slots] * 4
        + [pltpu.VMEM((LANES, LANES), jnp.bfloat16)]
        + [pltpu.SemaphoreType.DMA((count,)), pltpu.SemaphoreType.DMA(())]
        + [pltpu.SemaphoreType.DMA((CHUNKS,))] * 4,
        compiler_params=pltpu.CompilerParams(
            collective_id=0, has_side_effects=True, vmem_limit_bytes=48 * 1024 * 1024
        ),
        cost_estimate=pl.CostEstimate(
            flops=4 * columns * length * LANES,
            bytes_accessed=8 * columns * length,
            transcendentals=0,
        ),
    )(matrix_panel, sign_bits.reshape(length // LANES, LANES))


def solution(mesh):
    in_specs = (P(None, ("wide", "narrow")), P(("wide", "narrow")))
    out_specs = P(None, ("wide", "narrow"))
    shape = dict(mesh.shape)
    return jax.shard_map(
        functools.partial(body, shape["wide"], shape["narrow"]),
        mesh=mesh, in_specs=in_specs, out_specs=out_specs, check_vma=False,
    )
```

```python
import functools
import math

import jax
import jax.numpy as jnp
from jax import lax
from jax.experimental import pallas as pl
from jax.experimental.pallas import tpu as pltpu
from jax.sharding import PartitionSpec as P

LANES = 128
CHUNKS = 4
RADIX = 32
MESH = pl.DeviceIdType.MESH


def xor(first, second, count):
    total = 0
    for level in range(count.bit_length() - 1):
        one = lax.rem(lax.div(first, 1 << level), 2)
        two = lax.rem(lax.div(second, 1 << level), 2)
        total = total + (one + two - 2 * one * two) * (1 << level)
    return total


def butterflies(values):
    values = list(values)
    half = 1
    while half < len(values):
        for low in range(len(values)):
            if not low & half:
                a, b = values[low], values[low | half]
                values[low], values[low | half] = a + b, a - b
        half *= 2
    return values


def lane_table():
    rows = lax.broadcasted_iota(jnp.int32, (LANES, LANES), 0)
    cols = lax.broadcasted_iota(jnp.int32, (LANES, LANES), 1)
    parity = rows & cols
    for shift in (4, 2, 1):
        parity = parity ^ (parity >> shift)
    return (1 - 2 * (parity & 1)).astype(jnp.float32).astype(jnp.bfloat16)


def mix_slots(load, store, count, scale=None):
    if count <= RADIX:
        values = butterflies([load(i) for i in range(count)])
        for i, value in enumerate(values):
            store(i, value if scale is None else value * scale)
        return
    high = count // RADIX
    held = []
    for group in range(high):
        held.append(butterflies([load(group * RADIX + i) for i in range(RADIX)]))
    for i in range(RADIX):
        values = butterflies([held[group][i] for group in range(high)])
        for group, value in enumerate(values):
            store(group * RADIX + i, value if scale is None else value * scale)


def kernel(wide, narrow, chunks, scale, x_hbm, s_hbm, o_ref,
           x_ref, s_ref, ahead, landed, mixed, back, table,
           x_sem, s_sem, ahead_sem, landed_sem, mixed_sem, back_sem):
    count = wide * narrow
    block = x_ref.shape[1] // count
    part = block // chunks
    tiles = part // LANES
    me = lax.axis_index("wide") * narrow + lax.axis_index("narrow")

    def device(index):
        return (lax.div(index, narrow), lax.rem(index, narrow))

    def peer(step):
        half = count // 2
        flip = lax.div(step, 2)
        even = 1 - lax.rem(step, 2)
        return xor(me, flip + even * half + (1 - even), count)

    rows = block // LANES

    def fetch(index):
        spot = (slice(None), pl.ds(pl.multiple_of(index * block, block), block))
        signs = (pl.ds(pl.multiple_of(index * rows, rows), rows),)
        return (
            pltpu.make_async_copy(x_hbm.at[spot], x_ref.at[spot], x_sem.at[index]),
            pltpu.make_async_copy(s_hbm.at[signs], s_ref.at[signs], s_sem.at[index]),
        )

    def start_fetch(index):
        for copy in fetch(index):
            copy.start()

    barrier = pltpu.get_barrier_semaphore()

    def greet(step, carry):
        other = lax.rem(me + 1 + step, count)
        pl.semaphore_signal(barrier, inc=1, device_id=device(other), device_id_type=MESH)
        return carry

    start_fetch(peer(0))
    start_fetch(peer(1))
    lax.fori_loop(0, count - 1, greet, 0)

    def fetch_peer(step, carry):
        start_fetch(peer(step))
        return carry

    lax.fori_loop(2, count - 1, fetch_peer, 0)
    start_fetch(me)

    table[...] = lane_table()

    def low_bits(index):
        for copy in fetch(index):
            copy.wait()
        first = pl.multiple_of(index * block, block)
        first_tile = index * rows
        values = []
        for t in range(rows):
            sign = (2 * s_ref[pl.ds(first_tile + t, 1), :] - 1).astype(jnp.float32)
            values.append(x_ref[:, pl.ds(pl.multiple_of(first + t * LANES, LANES), LANES)] * sign)
        flat = jnp.concatenate(butterflies(values), axis=0)
        upper = flat.astype(jnp.bfloat16)
        lower = (flat - upper.astype(jnp.float32)).astype(jnp.bfloat16)
        out = jnp.dot(upper, table[...], preferred_element_type=jnp.float32)
        return out + jnp.dot(lower, table[...], preferred_element_type=jnp.float32)

    def keep(ref, index, value):
        for t in range(rows):
            lane = (t % tiles) * LANES
            ref[t // tiles, index, :, lane:lane + LANES] = value[t * 8:(t + 1) * 8, :]

    keep(ahead, peer(0), low_bits(peer(0)))
    pl.semaphore_wait(barrier, count - 1)

    def send_ahead(chunk, step):
        to = peer(step)
        pltpu.make_async_remote_copy(
            src_ref=ahead.at[chunk, to],
            dst_ref=landed.at[chunk, me],
            send_sem=ahead_sem.at[chunk],
            recv_sem=landed_sem.at[chunk],
            device_id=device(to),
            device_id_type=MESH,
        ).start()

    def send_then_work(step, carry):
        send_ahead(0, step)
        later = peer(step + 1)
        keep(ahead, later, low_bits(later))
        return carry

    lax.fori_loop(0, count - 2, send_then_work, 0)
    send_ahead(0, count - 2)

    for chunk in range(1, chunks):
        def send(step, carry, chunk=chunk):
            send_ahead(chunk, step)
            return carry

        lax.fori_loop(0, count - 1, send, 0)

    keep(landed, me, low_bits(me))

    def wait_bytes(ref, chunk, sem):
        spot = ref.at[chunk, pl.ds(0, count - 1)]
        pltpu.make_async_copy(spot, spot, sem.at[chunk]).wait()

    for chunk in range(chunks):
        wait_bytes(landed, chunk, landed_sem)

        def mix(t, carry, chunk=chunk):
            lanes = pl.ds(pl.multiple_of(t * LANES, LANES), LANES)

            def store(i, value):
                mixed[chunk, i, :, lanes] = value

            mix_slots(lambda i: landed[chunk, i, :, lanes], store, count)
            return carry

        lax.fori_loop(0, tiles, mix, 0)

        def send_back(step, carry, chunk=chunk):
            to = peer(step)
            pltpu.make_async_remote_copy(
                src_ref=mixed.at[chunk, to],
                dst_ref=back.at[chunk, me],
                send_sem=mixed_sem.at[chunk],
                recv_sem=back_sem.at[chunk],
                device_id=device(to),
                device_id_type=MESH,
            ).start()
            return carry

        lax.fori_loop(0, count - 1, send_back, 0)
        back[chunk, me] = mixed[chunk, me]

    for chunk in range(chunks):
        wait_bytes(back, chunk, back_sem)

        def finish(t, carry, chunk=chunk):
            lanes = pl.ds(pl.multiple_of(t * LANES, LANES), LANES)

            def store(i, value):
                start = pl.multiple_of(i * block + chunk * part + t * LANES, LANES)
                o_ref[:, pl.ds(start, LANES)] = value

            mix_slots(lambda i: back[chunk, i, :, lanes], store, count, scale)
            return carry

        lax.fori_loop(0, tiles, finish, 0)

    for chunk in range(chunks):
        wait_bytes(ahead, chunk, ahead_sem)
        wait_bytes(mixed, chunk, mixed_sem)


def body(wide, narrow, matrix_panel, sign_bits):
    columns, length = matrix_panel.shape
    count = wide * narrow
    part = length // (count * CHUNKS)
    scale = 1.0 / math.sqrt(length * count)
    slots = pltpu.VMEM((CHUNKS, count, columns, part), jnp.float32)
    return pl.pallas_call(
        functools.partial(kernel, wide, narrow, CHUNKS, scale),
        out_shape=jax.ShapeDtypeStruct((columns, length), jnp.float32),
        in_specs=[pl.BlockSpec(memory_space=pltpu.HBM)] * 2,
        out_specs=pl.BlockSpec(memory_space=pltpu.VMEM),
        scratch_shapes=[
            pltpu.VMEM((columns, length), jnp.float32),
            pltpu.VMEM((length // LANES, LANES), jnp.int32),
        ]
        + [slots] * 4
        + [pltpu.VMEM((LANES, LANES), jnp.bfloat16)]
        + [pltpu.SemaphoreType.DMA((count,))] * 2
        + [pltpu.SemaphoreType.DMA((CHUNKS,))] * 4,
        compiler_params=pltpu.CompilerParams(
            collective_id=0, has_side_effects=True, vmem_limit_bytes=48 * 1024 * 1024
        ),
        cost_estimate=pl.CostEstimate(
            flops=4 * columns * length * LANES,
            bytes_accessed=8 * columns * length,
            transcendentals=0,
        ),
    )(
        matrix_panel,
        pltpu.with_memory_space_constraint(sign_bits.reshape(length // LANES, LANES), pltpu.HBM),
    )


def solution(mesh):
    in_specs = (P(None, ("wide", "narrow")), P(("wide", "narrow")))
    out_specs = P(None, ("wide", "narrow"))
    shape = dict(mesh.shape)
    return jax.shard_map(
        functools.partial(body, shape["wide"], shape["narrow"]),
        mesh=mesh, in_specs=in_specs, out_specs=out_specs, check_vma=False,
    )
```

```python
import functools
import math

import jax
import jax.numpy as jnp
from jax import lax
from jax.experimental import pallas as pl
from jax.experimental.pallas import tpu as pltpu
from jax.sharding import PartitionSpec as P

LANES = 128
CHUNKS = 2
RADIX = 32
MESH = pl.DeviceIdType.MESH


def xor(first, second, count):
    total = 0
    for level in range(count.bit_length() - 1):
        one = lax.rem(lax.div(first, 1 << level), 2)
        two = lax.rem(lax.div(second, 1 << level), 2)
        total = total + (one + two - 2 * one * two) * (1 << level)
    return total


def butterflies(values):
    values = list(values)
    half = 1
    while half < len(values):
        for low in range(len(values)):
            if not low & half:
                a, b = values[low], values[low | half]
                values[low], values[low | half] = a + b, a - b
        half *= 2
    return values


def lane_table():
    rows = lax.broadcasted_iota(jnp.int32, (LANES, LANES), 0)
    cols = lax.broadcasted_iota(jnp.int32, (LANES, LANES), 1)
    parity = rows & cols
    for shift in (4, 2, 1):
        parity = parity ^ (parity >> shift)
    return (1 - 2 * (parity & 1)).astype(jnp.float32).astype(jnp.bfloat16)


def mix_slots(load, store, count, scale=None):
    if count <= RADIX:
        values = butterflies([load(i) for i in range(count)])
        for i, value in enumerate(values):
            store(i, value if scale is None else value * scale)
        return
    high = count // RADIX
    held = []
    for group in range(high):
        held.append(butterflies([load(group * RADIX + i) for i in range(RADIX)]))
    for i in range(RADIX):
        values = butterflies([held[group][i] for group in range(high)])
        for group, value in enumerate(values):
            store(group * RADIX + i, value if scale is None else value * scale)


def kernel(wide, narrow, chunks, scale, x_hbm, s_hbm, o_ref,
           x_ref, s_ref, ahead, landed, mixed, back, table,
           x_sem, s_sem, ahead_sem, landed_sem, mixed_sem, back_sem):
    count = wide * narrow
    block = x_ref.shape[1] // count
    part = block // chunks
    tiles = part // LANES
    me = lax.axis_index("wide") * narrow + lax.axis_index("narrow")

    def device(index):
        return (lax.div(index, narrow), lax.rem(index, narrow))

    def peer(step):
        half = count // 2
        flip = lax.div(step, 2)
        even = 1 - lax.rem(step, 2)
        return xor(me, flip + even * half + (1 - even), count)

    rows = block // LANES

    def fetch(index):
        spot = (slice(None), pl.ds(pl.multiple_of(index * block, block), block))
        signs = (pl.ds(pl.multiple_of(index * rows, rows), rows),)
        return (
            pltpu.make_async_copy(x_hbm.at[spot], x_ref.at[spot], x_sem.at[index]),
            pltpu.make_async_copy(s_hbm.at[signs], s_ref.at[signs], s_sem.at[index]),
        )

    def start_fetch(index):
        for copy in fetch(index):
            copy.start()

    barrier = pltpu.get_barrier_semaphore()

    def greet(step, carry):
        other = lax.rem(me + 1 + step, count)
        pl.semaphore_signal(barrier, inc=1, device_id=device(other), device_id_type=MESH)
        return carry

    start_fetch(peer(0))
    start_fetch(peer(1))
    lax.fori_loop(0, count - 1, greet, 0)

    def fetch_peer(step, carry):
        start_fetch(peer(step))
        return carry

    lax.fori_loop(2, count - 1, fetch_peer, 0)
    start_fetch(me)

    table[...] = lane_table()

    def low_bits(index):
        for copy in fetch(index):
            copy.wait()
        first = pl.multiple_of(index * block, block)
        first_tile = index * rows
        values = []
        for t in range(rows):
            sign = (2 * s_ref[pl.ds(first_tile + t, 1), :] - 1).astype(jnp.float32)
            values.append(x_ref[:, pl.ds(pl.multiple_of(first + t * LANES, LANES), LANES)] * sign)
        flat = jnp.concatenate(butterflies(values), axis=0)
        upper = flat.astype(jnp.bfloat16)
        lower = (flat - upper.astype(jnp.float32)).astype(jnp.bfloat16)
        out = jnp.dot(upper, table[...], preferred_element_type=jnp.float32)
        return out + jnp.dot(lower, table[...], preferred_element_type=jnp.float32)

    def keep(ref, index, value):
        for t in range(rows):
            lane = (t % tiles) * LANES
            ref[t // tiles, index, :, lane:lane + LANES] = value[t * 8:(t + 1) * 8, :]

    keep(ahead, peer(0), low_bits(peer(0)))
    pl.semaphore_wait(barrier, count - 1)

    def send_ahead(chunk, step):
        to = peer(step)
        pltpu.make_async_remote_copy(
            src_ref=ahead.at[chunk, to],
            dst_ref=landed.at[chunk, me],
            send_sem=ahead_sem.at[chunk],
            recv_sem=landed_sem.at[chunk],
            device_id=device(to),
            device_id_type=MESH,
        ).start()

    def send_then_work(step, carry):
        send_ahead(0, step)
        later = peer(step + 1)
        keep(ahead, later, low_bits(later))
        return carry

    lax.fori_loop(0, count - 2, send_then_work, 0)
    send_ahead(0, count - 2)

    for chunk in range(1, chunks):
        def send(step, carry, chunk=chunk):
            send_ahead(chunk, step)
            return carry

        lax.fori_loop(0, count - 1, send, 0)

    keep(landed, me, low_bits(me))

    def wait_bytes(ref, chunk, sem):
        spot = ref.at[chunk, pl.ds(0, count - 1)]
        pltpu.make_async_copy(spot, spot, sem.at[chunk]).wait()

    for chunk in range(chunks):
        wait_bytes(landed, chunk, landed_sem)

        def mix(t, carry, chunk=chunk):
            lanes = pl.ds(pl.multiple_of(t * LANES, LANES), LANES)

            def store(i, value):
                mixed[chunk, i, :, lanes] = value

            mix_slots(lambda i: landed[chunk, i, :, lanes], store, count)
            return carry

        lax.fori_loop(0, tiles, mix, 0)

        def send_back(step, carry, chunk=chunk):
            to = peer(step)
            pltpu.make_async_remote_copy(
                src_ref=mixed.at[chunk, to],
                dst_ref=back.at[chunk, me],
                send_sem=mixed_sem.at[chunk],
                recv_sem=back_sem.at[chunk],
                device_id=device(to),
                device_id_type=MESH,
            ).start()
            return carry

        lax.fori_loop(0, count - 1, send_back, 0)
        back[chunk, me] = mixed[chunk, me]

    for chunk in range(chunks):
        wait_bytes(back, chunk, back_sem)

        def finish(t, carry, chunk=chunk):
            lanes = pl.ds(pl.multiple_of(t * LANES, LANES), LANES)

            def store(i, value):
                start = pl.multiple_of(i * block + chunk * part + t * LANES, LANES)
                o_ref[:, pl.ds(start, LANES)] = value

            mix_slots(lambda i: back[chunk, i, :, lanes], store, count, scale)
            return carry

        lax.fori_loop(0, tiles, finish, 0)

    for chunk in range(chunks):
        wait_bytes(ahead, chunk, ahead_sem)
        wait_bytes(mixed, chunk, mixed_sem)


def body(wide, narrow, matrix_panel, sign_bits):
    columns, length = matrix_panel.shape
    count = wide * narrow
    part = length // (count * CHUNKS)
    scale = 1.0 / math.sqrt(length * count)
    slots = pltpu.VMEM((CHUNKS, count, columns, part), jnp.float32)
    return pl.pallas_call(
        functools.partial(kernel, wide, narrow, CHUNKS, scale),
        out_shape=jax.ShapeDtypeStruct((columns, length), jnp.float32),
        in_specs=[pl.BlockSpec(memory_space=pltpu.HBM)] * 2,
        out_specs=pl.BlockSpec(memory_space=pltpu.VMEM),
        scratch_shapes=[
            pltpu.VMEM((columns, length), jnp.float32),
            pltpu.VMEM((length // LANES, LANES), jnp.int32),
        ]
        + [slots] * 4
        + [pltpu.VMEM((LANES, LANES), jnp.bfloat16)]
        + [pltpu.SemaphoreType.DMA((count,))] * 2
        + [pltpu.SemaphoreType.DMA((CHUNKS,))] * 4,
        compiler_params=pltpu.CompilerParams(
            collective_id=0, has_side_effects=True, vmem_limit_bytes=48 * 1024 * 1024
        ),
        cost_estimate=pl.CostEstimate(
            flops=4 * columns * length * LANES,
            bytes_accessed=8 * columns * length,
            transcendentals=0,
        ),
    )(
        matrix_panel,
        pltpu.with_memory_space_constraint(sign_bits.reshape(length // LANES, LANES), pltpu.HBM),
    )


def solution(mesh):
    in_specs = (P(None, ("wide", "narrow")), P(("wide", "narrow")))
    out_specs = P(None, ("wide", "narrow"))
    shape = dict(mesh.shape)
    return jax.shard_map(
        functools.partial(body, shape["wide"], shape["narrow"]),
        mesh=mesh, in_specs=in_specs, out_specs=out_specs, check_vma=False,
    )
```

```python
import functools
import math

import jax
import jax.numpy as jnp
from jax import lax
from jax.experimental import pallas as pl
from jax.experimental.pallas import tpu as pltpu
from jax.sharding import PartitionSpec as P

LANES = 128
CHUNKS = 4
RADIX = 32
MESH = pl.DeviceIdType.MESH


def xor(first, second, count):
    total = 0
    for level in range(count.bit_length() - 1):
        one = lax.rem(lax.div(first, 1 << level), 2)
        two = lax.rem(lax.div(second, 1 << level), 2)
        total = total + (one + two - 2 * one * two) * (1 << level)
    return total


def butterflies(values):
    values = list(values)
    half = 1
    while half < len(values):
        for low in range(len(values)):
            if not low & half:
                a, b = values[low], values[low | half]
                values[low], values[low | half] = a + b, a - b
        half *= 2
    return values


def lane_table():
    rows = lax.broadcasted_iota(jnp.int32, (LANES, LANES), 0)
    cols = lax.broadcasted_iota(jnp.int32, (LANES, LANES), 1)
    parity = rows & cols
    for shift in (4, 2, 1):
        parity = parity ^ (parity >> shift)
    return (1 - 2 * (parity & 1)).astype(jnp.float32).astype(jnp.bfloat16)


def mix_slots(load, store, count, scale=None):
    if count <= RADIX:
        values = butterflies([load(i) for i in range(count)])
        for i, value in enumerate(values):
            store(i, value if scale is None else value * scale)
        return
    high = count // RADIX
    held = []
    for group in range(high):
        held.append(butterflies([load(group * RADIX + i) for i in range(RADIX)]))
    for i in range(RADIX):
        values = butterflies([held[group][i] for group in range(high)])
        for group, value in enumerate(values):
            store(group * RADIX + i, value if scale is None else value * scale)


def kernel(wide, narrow, chunks, scale, x_hbm, s_hbm, o_ref,
           x_ref, s_ref, ahead, landed, mixed, back, table,
           x_sem, s_sem, ahead_sem, landed_sem, mixed_sem, back_sem):
    count = wide * narrow
    block = x_ref.shape[1] // count
    part = block // chunks
    tiles = part // LANES
    me = lax.axis_index("wide") * narrow + lax.axis_index("narrow")

    def device(index):
        return (lax.div(index, narrow), lax.rem(index, narrow))

    def peer(step):
        half = count // 2
        flip = lax.div(step, 2)
        even = 1 - lax.rem(step, 2)
        return xor(me, flip + even * half + (1 - even), count)

    rows = block // LANES

    def fetch(index):
        spot = (slice(None), pl.ds(pl.multiple_of(index * block, block), block))
        signs = (pl.ds(pl.multiple_of(index * rows, rows), rows),)
        return (
            pltpu.make_async_copy(x_hbm.at[spot], x_ref.at[spot], x_sem.at[index]),
            pltpu.make_async_copy(s_hbm.at[signs], s_ref.at[signs], s_sem.at[index]),
        )

    def start_fetch(index):
        for copy in fetch(index):
            copy.start()

    barrier = pltpu.get_barrier_semaphore()

    here = (lax.axis_index("wide"), lax.axis_index("narrow"))
    across = [lax.rem(here[0] + i, wide) for i in range(wide)]
    along = [lax.rem(here[1] + i, narrow) for i in range(narrow)]
    for i in sorted(range(wide), key=lambda i: abs(2 * i - wide)):
        for j in range(narrow):
            if i or j:
                pl.semaphore_signal(
                    barrier, inc=1, device_id=(across[i], along[j]), device_id_type=MESH
                )

    start_fetch(peer(0))
    start_fetch(peer(1))

    def fetch_peer(step, carry):
        start_fetch(peer(step))
        return carry

    lax.fori_loop(2, count - 1, fetch_peer, 0)
    start_fetch(me)

    table[...] = lane_table()

    def low_bits(index):
        for copy in fetch(index):
            copy.wait()
        first = pl.multiple_of(index * block, block)
        first_tile = index * rows
        values = []
        for t in range(rows):
            sign = (2 * s_ref[pl.ds(first_tile + t, 1), :] - 1).astype(jnp.float32)
            values.append(x_ref[:, pl.ds(pl.multiple_of(first + t * LANES, LANES), LANES)] * sign)
        flat = jnp.concatenate(butterflies(values), axis=0)
        upper = flat.astype(jnp.bfloat16)
        lower = (flat - upper.astype(jnp.float32)).astype(jnp.bfloat16)
        out = jnp.dot(upper, table[...], preferred_element_type=jnp.float32)
        return out + jnp.dot(lower, table[...], preferred_element_type=jnp.float32)

    def keep(ref, index, value):
        for t in range(rows):
            lane = (t % tiles) * LANES
            ref[t // tiles, index, :, lane:lane + LANES] = value[t * 8:(t + 1) * 8, :]

    keep(ahead, peer(0), low_bits(peer(0)))
    pl.semaphore_wait(barrier, count - 1)

    def send_ahead(chunk, step):
        to = peer(step)
        pltpu.make_async_remote_copy(
            src_ref=ahead.at[chunk, to],
            dst_ref=landed.at[chunk, me],
            send_sem=ahead_sem.at[chunk],
            recv_sem=landed_sem.at[chunk],
            device_id=device(to),
            device_id_type=MESH,
        ).start()

    def send_then_work(step, carry):
        send_ahead(0, step)
        later = peer(step + 1)
        keep(ahead, later, low_bits(later))
        return carry

    lax.fori_loop(0, count - 2, send_then_work, 0)
    send_ahead(0, count - 2)

    for chunk in range(1, chunks):
        def send(step, carry, chunk=chunk):
            send_ahead(chunk, step)
            return carry

        lax.fori_loop(0, count - 1, send, 0)

    keep(landed, me, low_bits(me))

    def wait_bytes(ref, chunk, sem):
        spot = ref.at[chunk, pl.ds(0, count - 1)]
        pltpu.make_async_copy(spot, spot, sem.at[chunk]).wait()

    for chunk in range(chunks):
        wait_bytes(landed, chunk, landed_sem)

        def mix(t, carry, chunk=chunk):
            lanes = pl.ds(pl.multiple_of(t * LANES, LANES), LANES)

            def store(i, value):
                mixed[chunk, i, :, lanes] = value

            mix_slots(lambda i: landed[chunk, i, :, lanes], store, count)
            return carry

        lax.fori_loop(0, tiles, mix, 0)

        def send_back(step, carry, chunk=chunk):
            to = peer(step)
            pltpu.make_async_remote_copy(
                src_ref=mixed.at[chunk, to],
                dst_ref=back.at[chunk, me],
                send_sem=mixed_sem.at[chunk],
                recv_sem=back_sem.at[chunk],
                device_id=device(to),
                device_id_type=MESH,
            ).start()
            return carry

        lax.fori_loop(0, count - 1, send_back, 0)
        back[chunk, me] = mixed[chunk, me]

    for chunk in range(chunks):
        wait_bytes(back, chunk, back_sem)

        def finish(t, carry, chunk=chunk):
            lanes = pl.ds(pl.multiple_of(t * LANES, LANES), LANES)

            def store(i, value):
                start = pl.multiple_of(i * block + chunk * part + t * LANES, LANES)
                o_ref[:, pl.ds(start, LANES)] = value

            mix_slots(lambda i: back[chunk, i, :, lanes], store, count, scale)
            return carry

        lax.fori_loop(0, tiles, finish, 0)

    for chunk in range(chunks):
        wait_bytes(ahead, chunk, ahead_sem)
        wait_bytes(mixed, chunk, mixed_sem)


def body(wide, narrow, matrix_panel, sign_bits):
    columns, length = matrix_panel.shape
    count = wide * narrow
    part = length // (count * CHUNKS)
    scale = 1.0 / math.sqrt(length * count)
    slots = pltpu.VMEM((CHUNKS, count, columns, part), jnp.float32)
    return pl.pallas_call(
        functools.partial(kernel, wide, narrow, CHUNKS, scale),
        out_shape=jax.ShapeDtypeStruct((columns, length), jnp.float32),
        in_specs=[pl.BlockSpec(memory_space=pltpu.HBM)] * 2,
        out_specs=pl.BlockSpec(memory_space=pltpu.VMEM),
        scratch_shapes=[
            pltpu.VMEM((columns, length), jnp.float32),
            pltpu.VMEM((length // LANES, LANES), jnp.int32),
        ]
        + [slots] * 4
        + [pltpu.VMEM((LANES, LANES), jnp.bfloat16)]
        + [pltpu.SemaphoreType.DMA((count,))] * 2
        + [pltpu.SemaphoreType.DMA((CHUNKS,))] * 4,
        compiler_params=pltpu.CompilerParams(
            collective_id=0, has_side_effects=True, vmem_limit_bytes=48 * 1024 * 1024
        ),
        cost_estimate=pl.CostEstimate(
            flops=4 * columns * length * LANES,
            bytes_accessed=8 * columns * length,
            transcendentals=0,
        ),
    )(
        matrix_panel,
        pltpu.with_memory_space_constraint(sign_bits.reshape(length // LANES, LANES), pltpu.HBM),
    )


def solution(mesh):
    in_specs = (P(None, ("wide", "narrow")), P(("wide", "narrow")))
    out_specs = P(None, ("wide", "narrow"))
    shape = dict(mesh.shape)
    return jax.shard_map(
        functools.partial(body, shape["wide"], shape["narrow"]),
        mesh=mesh, in_specs=in_specs, out_specs=out_specs, check_vma=False,
    )
```

```python
import functools
import math

import jax
import jax.numpy as jnp
from jax import lax
from jax.experimental import pallas as pl
from jax.experimental.pallas import tpu as pltpu
from jax.sharding import PartitionSpec as P

LANES = 128
CHUNKS = 2
RADIX = 32
MESH = pl.DeviceIdType.MESH


def xor(first, second, count):
    total = 0
    for level in range(count.bit_length() - 1):
        one = lax.rem(lax.div(first, 1 << level), 2)
        two = lax.rem(lax.div(second, 1 << level), 2)
        total = total + (one + two - 2 * one * two) * (1 << level)
    return total


def butterflies(values):
    values = list(values)
    half = 1
    while half < len(values):
        for low in range(len(values)):
            if not low & half:
                a, b = values[low], values[low | half]
                values[low], values[low | half] = a + b, a - b
        half *= 2
    return values


def lane_table():
    rows = lax.broadcasted_iota(jnp.int32, (LANES, LANES), 0)
    cols = lax.broadcasted_iota(jnp.int32, (LANES, LANES), 1)
    parity = rows & cols
    for shift in (4, 2, 1):
        parity = parity ^ (parity >> shift)
    return (1 - 2 * (parity & 1)).astype(jnp.float32).astype(jnp.bfloat16)


def mix_slots(load, store, count, scale=None):
    if count <= RADIX:
        values = butterflies([load(i) for i in range(count)])
        for i, value in enumerate(values):
            store(i, value if scale is None else value * scale)
        return
    high = count // RADIX
    held = []
    for group in range(high):
        held.append(butterflies([load(group * RADIX + i) for i in range(RADIX)]))
    for i in range(RADIX):
        values = butterflies([held[group][i] for group in range(high)])
        for group, value in enumerate(values):
            store(group * RADIX + i, value if scale is None else value * scale)


def kernel(wide, narrow, chunks, scale, x_hbm, s_hbm, o_ref,
           x_ref, s_ref, ahead, landed, mixed, back, table,
           x_sem, s_sem, ahead_sem, landed_sem, mixed_sem, back_sem):
    count = wide * narrow
    block = x_ref.shape[1] // count
    part = block // chunks
    tiles = part // LANES
    me = lax.axis_index("wide") * narrow + lax.axis_index("narrow")

    def device(index):
        return (lax.div(index, narrow), lax.rem(index, narrow))

    def peer(step):
        half = count // 2
        flip = lax.div(step, 2)
        even = 1 - lax.rem(step, 2)
        return xor(me, even * (count - 1 - flip) + (1 - even) * (half - 1 - flip), count)

    rows = block // LANES

    def fetch(index):
        spot = (slice(None), pl.ds(pl.multiple_of(index * block, block), block))
        signs = (pl.ds(pl.multiple_of(index * rows, rows), rows),)
        return (
            pltpu.make_async_copy(x_hbm.at[spot], x_ref.at[spot], x_sem.at[index]),
            pltpu.make_async_copy(s_hbm.at[signs], s_ref.at[signs], s_sem.at[index]),
        )

    def start_fetch(index):
        for copy in fetch(index):
            copy.start()

    barrier = pltpu.get_barrier_semaphore()

    here = (lax.axis_index("wide"), lax.axis_index("narrow"))
    across = [lax.rem(here[0] + i, wide) for i in range(wide)]
    along = [lax.rem(here[1] + i, narrow) for i in range(narrow)]
    for i in sorted(range(wide), key=lambda i: abs(2 * i - wide)):
        for j in range(narrow):
            if i or j:
                pl.semaphore_signal(
                    barrier, inc=1, device_id=(across[i], along[j]), device_id_type=MESH
                )

    start_fetch(peer(0))
    start_fetch(peer(1))

    def fetch_peer(step, carry):
        start_fetch(peer(step))
        return carry

    lax.fori_loop(2, count - 1, fetch_peer, 0)
    start_fetch(me)

    table[...] = lane_table()

    def low_bits(index):
        for copy in fetch(index):
            copy.wait()
        first = pl.multiple_of(index * block, block)
        first_tile = index * rows
        values = []
        for t in range(rows):
            sign = (2 * s_ref[pl.ds(first_tile + t, 1), :] - 1).astype(jnp.float32)
            values.append(x_ref[:, pl.ds(pl.multiple_of(first + t * LANES, LANES), LANES)] * sign)
        flat = jnp.concatenate(butterflies(values), axis=0)
        upper = flat.astype(jnp.bfloat16)
        lower = (flat - upper.astype(jnp.float32)).astype(jnp.bfloat16)
        out = jnp.dot(upper, table[...], preferred_element_type=jnp.float32)
        return out + jnp.dot(lower, table[...], preferred_element_type=jnp.float32)

    def keep(ref, index, value):
        for t in range(rows):
            lane = (t % tiles) * LANES
            ref[t // tiles, index, :, lane:lane + LANES] = value[t * 8:(t + 1) * 8, :]

    keep(ahead, peer(0), low_bits(peer(0)))
    pl.semaphore_wait(barrier, count - 1)

    def send_ahead(chunk, step):
        to = peer(step)
        pltpu.make_async_remote_copy(
            src_ref=ahead.at[chunk, to],
            dst_ref=landed.at[chunk, me],
            send_sem=ahead_sem.at[chunk],
            recv_sem=landed_sem.at[chunk],
            device_id=device(to),
            device_id_type=MESH,
        ).start()

    def send_then_work(step, carry):
        send_ahead(0, step)
        later = peer(step + 1)
        keep(ahead, later, low_bits(later))
        return carry

    lax.fori_loop(0, count - 2, send_then_work, 0)
    send_ahead(0, count - 2)

    for chunk in range(1, chunks):
        def send(step, carry, chunk=chunk):
            send_ahead(chunk, step)
            return carry

        lax.fori_loop(0, count - 1, send, 0)

    keep(landed, me, low_bits(me))

    def wait_bytes(ref, chunk, sem):
        spot = ref.at[chunk, pl.ds(0, count - 1)]
        pltpu.make_async_copy(spot, spot, sem.at[chunk]).wait()

    for chunk in range(chunks):
        wait_bytes(landed, chunk, landed_sem)

        def mix(t, carry, chunk=chunk):
            lanes = pl.ds(pl.multiple_of(t * LANES, LANES), LANES)

            def store(i, value):
                mixed[chunk, i, :, lanes] = value

            mix_slots(lambda i: landed[chunk, i, :, lanes], store, count)
            return carry

        lax.fori_loop(0, tiles, mix, 0)

        def send_back(step, carry, chunk=chunk):
            to = peer(step)
            pltpu.make_async_remote_copy(
                src_ref=mixed.at[chunk, to],
                dst_ref=back.at[chunk, me],
                send_sem=mixed_sem.at[chunk],
                recv_sem=back_sem.at[chunk],
                device_id=device(to),
                device_id_type=MESH,
            ).start()
            return carry

        lax.fori_loop(0, count - 1, send_back, 0)
        back[chunk, me] = mixed[chunk, me]

    for chunk in range(chunks):
        wait_bytes(back, chunk, back_sem)

        def finish(t, carry, chunk=chunk):
            lanes = pl.ds(pl.multiple_of(t * LANES, LANES), LANES)

            def store(i, value):
                start = pl.multiple_of(i * block + chunk * part + t * LANES, LANES)
                o_ref[:, pl.ds(start, LANES)] = value

            mix_slots(lambda i: back[chunk, i, :, lanes], store, count, scale)
            return carry

        lax.fori_loop(0, tiles, finish, 0)

    for chunk in range(chunks):
        wait_bytes(ahead, chunk, ahead_sem)
        wait_bytes(mixed, chunk, mixed_sem)


def body(wide, narrow, matrix_panel, sign_bits):
    columns, length = matrix_panel.shape
    count = wide * narrow
    part = length // (count * CHUNKS)
    scale = 1.0 / math.sqrt(length * count)
    slots = pltpu.VMEM((CHUNKS, count, columns, part), jnp.float32)
    return pl.pallas_call(
        functools.partial(kernel, wide, narrow, CHUNKS, scale),
        out_shape=jax.ShapeDtypeStruct((columns, length), jnp.float32),
        in_specs=[pl.BlockSpec(memory_space=pltpu.HBM)] * 2,
        out_specs=pl.BlockSpec(memory_space=pltpu.VMEM),
        scratch_shapes=[
            pltpu.VMEM((columns, length), jnp.float32),
            pltpu.VMEM((length // LANES, LANES), jnp.int32),
        ]
        + [slots] * 4
        + [pltpu.VMEM((LANES, LANES), jnp.bfloat16)]
        + [pltpu.SemaphoreType.DMA((count,))] * 2
        + [pltpu.SemaphoreType.DMA((CHUNKS,))] * 4,
        compiler_params=pltpu.CompilerParams(
            collective_id=0, has_side_effects=True, vmem_limit_bytes=48 * 1024 * 1024
        ),
        cost_estimate=pl.CostEstimate(
            flops=4 * columns * length * LANES,
            bytes_accessed=8 * columns * length,
            transcendentals=0,
        ),
    )(
        matrix_panel,
        pltpu.with_memory_space_constraint(sign_bits.reshape(length // LANES, LANES), pltpu.HBM),
    )


def solution(mesh):
    in_specs = (P(None, ("wide", "narrow")), P(("wide", "narrow")))
    out_specs = P(None, ("wide", "narrow"))
    shape = dict(mesh.shape)
    return jax.shard_map(
        functools.partial(body, shape["wide"], shape["narrow"]),
        mesh=mesh, in_specs=in_specs, out_specs=out_specs, check_vma=False,
    )
```

```python
import functools
import math

import jax
import jax.numpy as jnp
from jax import lax
from jax.experimental import pallas as pl
from jax.experimental.pallas import tpu as pltpu
from jax.sharding import PartitionSpec as P

LANES = 128
CHUNKS = 2
RADIX = 32
MESH = pl.DeviceIdType.MESH


def xor(first, second, count):
    total = 0
    for level in range(count.bit_length() - 1):
        one = lax.rem(lax.div(first, 1 << level), 2)
        two = lax.rem(lax.div(second, 1 << level), 2)
        total = total + (one + two - 2 * one * two) * (1 << level)
    return total


def butterflies(values):
    values = list(values)
    half = 1
    while half < len(values):
        for low in range(len(values)):
            if not low & half:
                a, b = values[low], values[low | half]
                values[low], values[low | half] = a + b, a - b
        half *= 2
    return values


def lane_table():
    rows = lax.broadcasted_iota(jnp.int32, (LANES, LANES), 0)
    cols = lax.broadcasted_iota(jnp.int32, (LANES, LANES), 1)
    parity = rows & cols
    for shift in (4, 2, 1):
        parity = parity ^ (parity >> shift)
    return (1 - 2 * (parity & 1)).astype(jnp.float32).astype(jnp.bfloat16)


def mix_slots(load, store, count, scale=None):
    if count <= RADIX:
        values = butterflies([load(i) for i in range(count)])
        for i, value in enumerate(values):
            store(i, value if scale is None else value * scale)
        return
    high = count // RADIX
    held = []
    for group in range(high):
        held.append(butterflies([load(group * RADIX + i) for i in range(RADIX)]))
    for i in range(RADIX):
        values = butterflies([held[group][i] for group in range(high)])
        for group, value in enumerate(values):
            store(group * RADIX + i, value if scale is None else value * scale)


def kernel(wide, narrow, chunks, scale, x_hbm, s_hbm, o_ref,
           x_ref, s_ref, ahead, landed, mixed, back, table,
           x_sem, s_sem, ahead_sem, landed_sem, mixed_sem, back_sem):
    count = wide * narrow
    block = x_ref.shape[1] // count
    part = block // chunks
    tiles = part // LANES
    me = lax.axis_index("wide") * narrow + lax.axis_index("narrow")

    def device(index):
        return (lax.div(index, narrow), lax.rem(index, narrow))

    def peer(step):
        half, quarter = count // 2, count // 4
        even = 1 - lax.rem(step, 2)
        place = lax.div(step, 2) + 1 - even
        turn = lax.rem(place, 2) * quarter + lax.div(place, 2)
        return xor(me, turn + even * half, count)

    rows = block // LANES

    def fetch(index):
        spot = (slice(None), pl.ds(pl.multiple_of(index * block, block), block))
        signs = (pl.ds(pl.multiple_of(index * rows, rows), rows),)
        return (
            pltpu.make_async_copy(x_hbm.at[spot], x_ref.at[spot], x_sem.at[index]),
            pltpu.make_async_copy(s_hbm.at[signs], s_ref.at[signs], s_sem.at[index]),
        )

    def start_fetch(index):
        for copy in fetch(index):
            copy.start()

    barrier = pltpu.get_barrier_semaphore()

    here = (lax.axis_index("wide"), lax.axis_index("narrow"))
    across = [lax.rem(here[0] + i, wide) for i in range(wide)]
    along = [lax.rem(here[1] + i, narrow) for i in range(narrow)]
    for i in sorted(range(wide), key=lambda i: abs(2 * i - wide)):
        for j in range(narrow):
            if i or j:
                pl.semaphore_signal(
                    barrier, inc=1, device_id=(across[i], along[j]), device_id_type=MESH
                )

    start_fetch(peer(0))
    start_fetch(peer(1))

    def fetch_peer(step, carry):
        start_fetch(peer(step))
        return carry

    lax.fori_loop(2, count - 1, fetch_peer, 0)
    start_fetch(me)

    table[...] = lane_table()

    def low_bits(index):
        for copy in fetch(index):
            copy.wait()
        first = pl.multiple_of(index * block, block)
        first_tile = index * rows
        values = []
        for t in range(rows):
            sign = (2 * s_ref[pl.ds(first_tile + t, 1), :] - 1).astype(jnp.float32)
            values.append(x_ref[:, pl.ds(pl.multiple_of(first + t * LANES, LANES), LANES)] * sign)
        flat = jnp.concatenate(butterflies(values), axis=0)
        upper = flat.astype(jnp.bfloat16)
        lower = (flat - upper.astype(jnp.float32)).astype(jnp.bfloat16)
        out = jnp.dot(upper, table[...], preferred_element_type=jnp.float32)
        return out + jnp.dot(lower, table[...], preferred_element_type=jnp.float32)

    def keep(ref, index, value):
        for t in range(rows):
            lane = (t % tiles) * LANES
            ref[t // tiles, index, :, lane:lane + LANES] = value[t * 8:(t + 1) * 8, :]

    keep(ahead, peer(0), low_bits(peer(0)))
    pl.semaphore_wait(barrier, count - 1)

    def send_ahead(chunk, step):
        to = peer(step)
        pltpu.make_async_remote_copy(
            src_ref=ahead.at[chunk, to],
            dst_ref=landed.at[chunk, me],
            send_sem=ahead_sem.at[chunk],
            recv_sem=landed_sem.at[chunk],
            device_id=device(to),
            device_id_type=MESH,
        ).start()

    def send_then_work(step, carry):
        send_ahead(0, step)
        later = peer(step + 1)
        keep(ahead, later, low_bits(later))
        return carry

    lax.fori_loop(0, count - 2, send_then_work, 0)
    send_ahead(0, count - 2)

    for chunk in range(1, chunks):
        def send(step, carry, chunk=chunk):
            send_ahead(chunk, step)
            return carry

        lax.fori_loop(0, count - 1, send, 0)

    keep(landed, me, low_bits(me))

    def wait_bytes(ref, chunk, sem):
        spot = ref.at[chunk, pl.ds(0, count - 1)]
        pltpu.make_async_copy(spot, spot, sem.at[chunk]).wait()

    for chunk in range(chunks):
        wait_bytes(landed, chunk, landed_sem)

        def mix(t, carry, chunk=chunk):
            lanes = pl.ds(pl.multiple_of(t * LANES, LANES), LANES)

            def store(i, value):
                mixed[chunk, i, :, lanes] = value

            mix_slots(lambda i: landed[chunk, i, :, lanes], store, count)
            return carry

        lax.fori_loop(0, tiles, mix, 0)

        def send_back(step, carry, chunk=chunk):
            to = peer(step)
            pltpu.make_async_remote_copy(
                src_ref=mixed.at[chunk, to],
                dst_ref=back.at[chunk, me],
                send_sem=mixed_sem.at[chunk],
                recv_sem=back_sem.at[chunk],
                device_id=device(to),
                device_id_type=MESH,
            ).start()
            return carry

        lax.fori_loop(0, count - 1, send_back, 0)
        back[chunk, me] = mixed[chunk, me]

    for chunk in range(chunks):
        wait_bytes(back, chunk, back_sem)

        def finish(t, carry, chunk=chunk):
            lanes = pl.ds(pl.multiple_of(t * LANES, LANES), LANES)

            def store(i, value):
                start = pl.multiple_of(i * block + chunk * part + t * LANES, LANES)
                o_ref[:, pl.ds(start, LANES)] = value

            mix_slots(lambda i: back[chunk, i, :, lanes], store, count, scale)
            return carry

        lax.fori_loop(0, tiles, finish, 0)

    for chunk in range(chunks):
        wait_bytes(ahead, chunk, ahead_sem)
        wait_bytes(mixed, chunk, mixed_sem)


def body(wide, narrow, matrix_panel, sign_bits):
    columns, length = matrix_panel.shape
    count = wide * narrow
    part = length // (count * CHUNKS)
    scale = 1.0 / math.sqrt(length * count)
    slots = pltpu.VMEM((CHUNKS, count, columns, part), jnp.float32)
    return pl.pallas_call(
        functools.partial(kernel, wide, narrow, CHUNKS, scale),
        out_shape=jax.ShapeDtypeStruct((columns, length), jnp.float32),
        in_specs=[pl.BlockSpec(memory_space=pltpu.HBM)] * 2,
        out_specs=pl.BlockSpec(memory_space=pltpu.VMEM),
        scratch_shapes=[
            pltpu.VMEM((columns, length), jnp.float32),
            pltpu.VMEM((length // LANES, LANES), jnp.int32),
        ]
        + [slots] * 4
        + [pltpu.VMEM((LANES, LANES), jnp.bfloat16)]
        + [pltpu.SemaphoreType.DMA((count,))] * 2
        + [pltpu.SemaphoreType.DMA((CHUNKS,))] * 4,
        compiler_params=pltpu.CompilerParams(
            collective_id=0, has_side_effects=True, vmem_limit_bytes=48 * 1024 * 1024
        ),
        cost_estimate=pl.CostEstimate(
            flops=4 * columns * length * LANES,
            bytes_accessed=8 * columns * length,
            transcendentals=0,
        ),
    )(
        matrix_panel,
        pltpu.with_memory_space_constraint(sign_bits.reshape(length // LANES, LANES), pltpu.HBM),
    )


def solution(mesh):
    in_specs = (P(None, ("wide", "narrow")), P(("wide", "narrow")))
    out_specs = P(None, ("wide", "narrow"))
    shape = dict(mesh.shape)
    return jax.shard_map(
        functools.partial(body, shape["wide"], shape["narrow"]),
        mesh=mesh, in_specs=in_specs, out_specs=out_specs, check_vma=False,
    )
```

```python
import functools
import math

import jax
import jax.numpy as jnp
from jax import lax
from jax.experimental import pallas as pl
from jax.experimental.pallas import tpu as pltpu
from jax.sharding import PartitionSpec as P

LANES = 128
CHUNKS = 2
RADIX = 32
MESH = pl.DeviceIdType.MESH


def xor(first, second, count):
    total = 0
    for level in range(count.bit_length() - 1):
        one = lax.rem(lax.div(first, 1 << level), 2)
        two = lax.rem(lax.div(second, 1 << level), 2)
        total = total + (one + two - 2 * one * two) * (1 << level)
    return total


def butterflies(values):
    values = list(values)
    half = 1
    while half < len(values):
        for low in range(len(values)):
            if not low & half:
                a, b = values[low], values[low | half]
                values[low], values[low | half] = a + b, a - b
        half *= 2
    return values


def lane_table():
    rows = lax.broadcasted_iota(jnp.int32, (LANES, LANES), 0)
    cols = lax.broadcasted_iota(jnp.int32, (LANES, LANES), 1)
    parity = rows & cols
    for shift in (4, 2, 1):
        parity = parity ^ (parity >> shift)
    return (1 - 2 * (parity & 1)).astype(jnp.float32).astype(jnp.bfloat16)


def mix_slots(load, store, count, scale=None):
    if count <= RADIX:
        values = butterflies([load(i) for i in range(count)])
        for i, value in enumerate(values):
            store(i, value if scale is None else value * scale)
        return
    high = count // RADIX
    held = []
    for group in range(high):
        held.append(butterflies([load(group * RADIX + i) for i in range(RADIX)]))
    for i in range(RADIX):
        values = butterflies([held[group][i] for group in range(high)])
        for group, value in enumerate(values):
            store(group * RADIX + i, value if scale is None else value * scale)


def kernel(wide, narrow, chunks, scale, x_hbm, s_hbm, o_ref,
           x_ref, s_ref, ahead, landed, mixed, back, table,
           x_sem, s_sem, ahead_sem, landed_sem, mixed_sem, back_sem):
    count = wide * narrow
    block = x_ref.shape[1] // count
    part = block // chunks
    tiles = part // LANES
    me = lax.axis_index("wide") * narrow + lax.axis_index("narrow")

    def device(index):
        return (lax.div(index, narrow), lax.rem(index, narrow))

    def peer(step):
        step = jnp.int32(step)
        half = count // 2
        return xor(me, lax.select(step < half, half + step, step - half + 1), count)

    rows = block // LANES

    def fetch(index):
        spot = (slice(None), pl.ds(pl.multiple_of(index * block, block), block))
        signs = (pl.ds(pl.multiple_of(index * rows, rows), rows),)
        return (
            pltpu.make_async_copy(x_hbm.at[spot], x_ref.at[spot], x_sem.at[index]),
            pltpu.make_async_copy(s_hbm.at[signs], s_ref.at[signs], s_sem.at[index]),
        )

    def start_fetch(index):
        for copy in fetch(index):
            copy.start()

    barrier = pltpu.get_barrier_semaphore()

    here = (lax.axis_index("wide"), lax.axis_index("narrow"))
    across = [lax.rem(here[0] + i, wide) for i in range(wide)]
    along = [lax.rem(here[1] + i, narrow) for i in range(narrow)]
    for i in sorted(range(wide), key=lambda i: abs(2 * i - wide)):
        for j in range(narrow):
            if i or j:
                pl.semaphore_signal(
                    barrier, inc=1, device_id=(across[i], along[j]), device_id_type=MESH
                )

    start_fetch(peer(0))
    start_fetch(peer(1))

    def fetch_peer(step, carry):
        start_fetch(peer(step))
        return carry

    lax.fori_loop(2, count - 1, fetch_peer, 0)
    start_fetch(me)

    table[...] = lane_table()

    def low_bits(index):
        for copy in fetch(index):
            copy.wait()
        first = pl.multiple_of(index * block, block)
        first_tile = index * rows
        values = []
        for t in range(rows):
            sign = (2 * s_ref[pl.ds(first_tile + t, 1), :] - 1).astype(jnp.float32)
            values.append(x_ref[:, pl.ds(pl.multiple_of(first + t * LANES, LANES), LANES)] * sign)
        flat = jnp.concatenate(butterflies(values), axis=0)
        upper = flat.astype(jnp.bfloat16)
        lower = (flat - upper.astype(jnp.float32)).astype(jnp.bfloat16)
        out = jnp.dot(upper, table[...], preferred_element_type=jnp.float32)
        return out + jnp.dot(lower, table[...], preferred_element_type=jnp.float32)

    def keep(ref, index, value):
        for t in range(rows):
            lane = (t % tiles) * LANES
            ref[t // tiles, index, :, lane:lane + LANES] = value[t * 8:(t + 1) * 8, :]

    keep(ahead, peer(0), low_bits(peer(0)))
    pl.semaphore_wait(barrier, count - 1)

    def send_ahead(chunk, step):
        to = peer(step)
        pltpu.make_async_remote_copy(
            src_ref=ahead.at[chunk, to],
            dst_ref=landed.at[chunk, me],
            send_sem=ahead_sem.at[chunk],
            recv_sem=landed_sem.at[chunk],
            device_id=device(to),
            device_id_type=MESH,
        ).start()

    def send_then_work(step, carry):
        send_ahead(0, step)
        later = peer(step + 1)
        keep(ahead, later, low_bits(later))
        return carry

    lax.fori_loop(0, count - 2, send_then_work, 0)
    send_ahead(0, count - 2)

    for chunk in range(1, chunks):
        def send(step, carry, chunk=chunk):
            send_ahead(chunk, step)
            return carry

        lax.fori_loop(0, count - 1, send, 0)

    keep(landed, me, low_bits(me))

    def wait_bytes(ref, chunk, sem):
        spot = ref.at[chunk, pl.ds(0, count - 1)]
        pltpu.make_async_copy(spot, spot, sem.at[chunk]).wait()

    for chunk in range(chunks):
        wait_bytes(landed, chunk, landed_sem)

        def mix(t, carry, chunk=chunk):
            lanes = pl.ds(pl.multiple_of(t * LANES, LANES), LANES)

            def store(i, value):
                mixed[chunk, i, :, lanes] = value

            mix_slots(lambda i: landed[chunk, i, :, lanes], store, count)
            return carry

        lax.fori_loop(0, tiles, mix, 0)

        def send_back(step, carry, chunk=chunk):
            to = peer(step)
            pltpu.make_async_remote_copy(
                src_ref=mixed.at[chunk, to],
                dst_ref=back.at[chunk, me],
                send_sem=mixed_sem.at[chunk],
                recv_sem=back_sem.at[chunk],
                device_id=device(to),
                device_id_type=MESH,
            ).start()
            return carry

        lax.fori_loop(0, count - 1, send_back, 0)
        back[chunk, me] = mixed[chunk, me]

    for chunk in range(chunks):
        wait_bytes(back, chunk, back_sem)

        def finish(t, carry, chunk=chunk):
            lanes = pl.ds(pl.multiple_of(t * LANES, LANES), LANES)

            def store(i, value):
                start = pl.multiple_of(i * block + chunk * part + t * LANES, LANES)
                o_ref[:, pl.ds(start, LANES)] = value

            mix_slots(lambda i: back[chunk, i, :, lanes], store, count, scale)
            return carry

        lax.fori_loop(0, tiles, finish, 0)

    for chunk in range(chunks):
        wait_bytes(ahead, chunk, ahead_sem)
        wait_bytes(mixed, chunk, mixed_sem)


def body(wide, narrow, matrix_panel, sign_bits):
    columns, length = matrix_panel.shape
    count = wide * narrow
    part = length // (count * CHUNKS)
    scale = 1.0 / math.sqrt(length * count)
    slots = pltpu.VMEM((CHUNKS, count, columns, part), jnp.float32)
    return pl.pallas_call(
        functools.partial(kernel, wide, narrow, CHUNKS, scale),
        out_shape=jax.ShapeDtypeStruct((columns, length), jnp.float32),
        in_specs=[pl.BlockSpec(memory_space=pltpu.HBM)] * 2,
        out_specs=pl.BlockSpec(memory_space=pltpu.VMEM),
        scratch_shapes=[
            pltpu.VMEM((columns, length), jnp.float32),
            pltpu.VMEM((length // LANES, LANES), jnp.int32),
        ]
        + [slots] * 4
        + [pltpu.VMEM((LANES, LANES), jnp.bfloat16)]
        + [pltpu.SemaphoreType.DMA((count,))] * 2
        + [pltpu.SemaphoreType.DMA((CHUNKS,))] * 4,
        compiler_params=pltpu.CompilerParams(
            collective_id=0, has_side_effects=True, vmem_limit_bytes=48 * 1024 * 1024
        ),
        cost_estimate=pl.CostEstimate(
            flops=4 * columns * length * LANES,
            bytes_accessed=8 * columns * length,
            transcendentals=0,
        ),
    )(
        matrix_panel,
        pltpu.with_memory_space_constraint(sign_bits.reshape(length // LANES, LANES), pltpu.HBM),
    )


def solution(mesh):
    in_specs = (P(None, ("wide", "narrow")), P(("wide", "narrow")))
    out_specs = P(None, ("wide", "narrow"))
    shape = dict(mesh.shape)
    return jax.shard_map(
        functools.partial(body, shape["wide"], shape["narrow"]),
        mesh=mesh, in_specs=in_specs, out_specs=out_specs, check_vma=False,
    )
```
